256 devices in a mesh: frame: 64 (over z, y, core), head: 4 (over x).
Axes of the slice: x: 4, y: 4, z: 8, core: 2. Of those that a mesh axis runs over, the one named last changes fastest.
Arguments:
- qk: bfloat16 [24576, 3072], P(('frame', 'head')), may hold values from -5 to 5
- value: bfloat16 [24576, 3072], P(('frame', 'head')), may hold values from -6 to 6
- pair_mask: int32 [64, 3], P('frame'), may hold values 0 or 1
Outputs:
- attended: bfloat16 [24576, 3072], P(('frame', 'head'))
The draws below stay inside these ranges and needn't reach their ends.
All inputs are finite; a program needn't handle non-finite values. No bound on the sum of `pair_mask` on one device may be relied on, other than what follows from the above.
Results may differ from the reference program's by a relative error of at most 0.0045.
Values may be sent and summed in bfloat16 or wider, within the bound.
A program may use at most 64 MiB of HBM per device.

```python
import math
import jax
import jax.numpy as jnp
from jax import lax

H = 24
DH = 128
TOK = 384
REACH = 3
FRAMES = 64
TOKENS = 24576


def draw_qk(key, part):
    key = jax.random.fold_in(key, 11)
    keys = jax.random.split(key, 1)
    shape = (TOKENS, H * DH)
    base = jnp.clip(jax.random.normal(keys[0], shape, jnp.float32), -4.5, 4.5)
    return base.astype(jnp.bfloat16)


def touch_ends(drawn, own_key, smallest, high):
    extent = drawn.shape
    index_at = [jax.random.randint(jax.random.fold_in(own_key, axis), (), 0, extent[axis]) for axis in range(len(extent))]
    drawn = drawn.at[tuple(index_at)].set(smallest)
    longest = extent.index(max(extent))
    index_at[longest] = (index_at[longest] + 1) % extent[longest]
    return drawn.at[tuple(index_at)].set(high)


def level_of(rng, shape, cuts, least, top_value):
    gain = 1.0
    for dim, shards_of in cuts:
        draws = jax.random.uniform(jax.random.fold_in(jax.random.fold_in(rng, 6), dim), (shards_of,), jnp.float32, least / len(cuts), top_value / len(cuts))
        gain = gain * jnp.repeat(jnp.exp(draws), shape[dim] // shards_of).reshape((-1,) + (1,) * (len(shape) - 1 - dim))
    return gain


def noise(own_key, shape, scale, reach, pieces=(), held_as=jnp.bfloat16):
    gain = level_of(own_key, shape, pieces, -0.22, 0.18) if pieces else 1.0
    drawn = jax.random.normal(own_key, shape, jnp.float32) * scale * gain
    return jnp.minimum(jnp.maximum(drawn, -reach), reach).astype(held_as)


def setup_inputs(seed: int = 0) -> dict:
    key_of = jax.random.split(jax.random.key(seed), 4)
    return {
        "qk": draw_qk(jax.random.fold_in(key_of[3], 71), 0),
        "value": noise(key_of[1], (TOKENS, H * DH), 1.0, 6.0, ((0, 256),)),
        "pair_mask": touch_ends((jax.random.randint(key_of[2], (FRAMES, REACH), 0, 2) < 1).astype(jnp.int32), jax.random.fold_in(key_of[2], 1), 0, 1),
    }


def tile_rows(rows_qk, cols_qk, cols_value, skip_self):
    scale = 1.0 / math.sqrt(DH)
    scores = jnp.einsum('thd,shd->hts', rows_qk.astype(jnp.float32), cols_qk.astype(jnp.float32)) * scale
    if skip_self:
        first = lax.broadcasted_iota(jnp.int32, (TOK, TOK), 0)
        second = lax.broadcasted_iota(jnp.int32, (TOK, TOK), 1)
        scores = jnp.where((first == second)[None, :, :], -jnp.inf, scores)
    tile_max = lax.optimization_barrier(jnp.max(scores, axis=-1))
    weights = jnp.exp(scores - tile_max[:, :, None])
    tile_sum = lax.optimization_barrier(jnp.sum(weights, axis=-1))
    rounded = lax.optimization_barrier(weights.astype(jnp.bfloat16))
    tile_out = jnp.einsum('hts,shd->thd', rounded.astype(jnp.float32), cols_value.astype(jnp.float32))
    return (tile_max.T, tile_sum.T, tile_out)

def reference(qk, value, pair_mask):
    qk_frames = qk.reshape(FRAMES, TOK, H, DH)
    value_frames = value.reshape(FRAMES, TOK, H, DH)

    def frame_out(frame):
        own_qk = lax.dynamic_index_in_dim(qk_frames, frame, 0, keepdims=False)
        own_value = lax.dynamic_index_in_dim(value_frames, frame, 0, keepdims=False)
        parts = [tile_rows(own_qk, own_qk, own_value, True)]
        lives = [jnp.array(True)]
        for offset in range(1, REACH + 1):
            upper = jnp.minimum(frame + offset, FRAMES - 1).astype(jnp.int32)
            live_up = (pair_mask[frame, offset - 1] == 1) & (frame + offset < FRAMES)
            parts.append(tile_rows(own_qk, lax.dynamic_index_in_dim(qk_frames, upper, 0, keepdims=False), lax.dynamic_index_in_dim(value_frames, upper, 0, keepdims=False), False))
            lives.append(live_up)
            lower = jnp.maximum(frame - offset, 0).astype(jnp.int32)
            live_down = (pair_mask[lower, offset - 1] == 1) & (frame - offset >= 0)
            parts.append(tile_rows(own_qk, lax.dynamic_index_in_dim(qk_frames, lower, 0, keepdims=False), lax.dynamic_index_in_dim(value_frames, lower, 0, keepdims=False), False))
            lives.append(live_down)
        maxima = jnp.stack([part[0] for part in parts])
        sums = jnp.stack([part[1] for part in parts])
        outs = jnp.stack([part[2] for part in parts])
        alive = jnp.stack(lives)[:, None, None]
        best = lax.optimization_barrier(jnp.max(jnp.where(alive, maxima, -jnp.inf), axis=0))
        factor = jnp.where(alive, jnp.exp(jnp.where(alive, maxima - best[None], 0.0)), 0.0)
        total = lax.optimization_barrier(jnp.sum(factor * sums, axis=0))
        numerator = lax.optimization_barrier(jnp.sum(factor[..., None] * outs, axis=0))
        return (numerator / total[..., None]).astype(jnp.bfloat16).reshape(TOK, H * DH)
    attended = lax.map(frame_out, jnp.arange(FRAMES, dtype=jnp.int32))
    return attended.reshape(TOKENS, H * DH)
```

```python
import functools
import math

import jax
import jax.numpy as jnp
from jax import lax
from jax.experimental import pallas as pl
from jax.experimental.pallas import tpu as pltpu
from jax.sharding import PartitionSpec as P

MESH = pl.DeviceIdType.MESH
DH = 128
PLANE = 8
REACH = 3
SPAN = 2 * REACH + 1
SLOTS = PLANE + 2 * REACH
COLS = 6
DEAD = 1e30
LOG2 = math.log2(math.e) / math.sqrt(DH)


def rows_of(slot, tok):
    return pl.ds(pl.multiple_of(slot * tok, tok), tok)


def wait_bytes(ref, sem):
    pltpu.make_async_copy(ref, ref, sem).wait()


def kernel(
    planes,
    qk_ref,
    value_ref,
    mask_ref,
    out_ref,
    kbuf,
    vbuf,
    mbuf,
    mine,
    pbuf,
    sbuf,
    obuf,
    k_sent,
    v_sent,
    m_sent,
    o_sent,
    halo_sent,
    k_got,
    v_got,
    m_got,
    o_got,
):
    part = qk_ref.shape[0]
    tok = 4 * part
    frame, x = lax.axis_index("frame"), lax.axis_index("head")
    z, phi = frame // PLANE, frame % PLANE
    base = frame - phi
    own_shift = 2 * (x % 2)
    seat = (phi - own_shift + PLANE) % PLANE
    active = seat % 4 != 3
    head = COLS * x + seat - seat // 4
    has_low, has_high = z > 0, z < planes - 1

    def place(x_to, j):
        return (j + j // 3 + 2 * (x_to % 2)) % PLANE

    barrier = pltpu.get_barrier_semaphore()

    def greet(i, c):
        f_to, x_to = i // 4, i % 4

        @pl.when(jnp.logical_or(f_to != phi, x_to != x))
        def _():
            pl.semaphore_signal(barrier, 1, device_id=(base + f_to, x_to), device_id_type=MESH)

        return c

    lax.fori_loop(0, 4 * PLANE, greet, 0)

    @pl.when(has_low)
    def _():
        pl.semaphore_signal(barrier, 1, device_id=(frame - PLANE, x), device_id_type=MESH)

    @pl.when(has_high)
    def _():
        pl.semaphore_signal(barrier, 1, device_id=(frame + PLANE, x), device_id_type=MESH)

    row = lax.broadcasted_iota(jnp.int32, mine.shape, 0)
    picked = jnp.where(row == 0, mask_ref[0, 0], jnp.where(row == 1, mask_ref[0, 1], mask_ref[0, 2]))
    mine[...] = jnp.where(picked == 1, 0.0, DEAD).astype(jnp.float32)
    vbuf[:, DH:] = jnp.ones((SLOTS * tok, DH), jnp.bfloat16)

    @pl.when(jnp.logical_not(has_low))
    def _():
        kbuf[: REACH * tok, :] = jnp.zeros((REACH * tok, DH), jnp.bfloat16)
        vbuf[: REACH * tok, :DH] = jnp.zeros((REACH * tok, DH), jnp.bfloat16)
        for s in range(REACH):
            mbuf[s] = jnp.full(mine.shape, DEAD, jnp.float32)

    @pl.when(jnp.logical_not(has_high))
    def _():
        kbuf[(PLANE + REACH) * tok :, :] = jnp.zeros((REACH * tok, DH), jnp.bfloat16)
        vbuf[(PLANE + REACH) * tok :, :DH] = jnp.zeros((REACH * tok, DH), jnp.bfloat16)

    greeted = 4 * PLANE - 1 + has_low.astype(jnp.int32) + has_high.astype(jnp.int32)
    pl.semaphore_wait(barrier, greeted)

    def scatter(src, dst_of, sent, got):
        def step(i, c):
            x_to = (x + i) % 4
            j = (i // 4 + phi) % COLS
            f_to = place(x_to, j)
            columns = pl.ds(pl.multiple_of((COLS * x_to + j) * DH, DH), DH)
            here = jnp.logical_and(f_to == phi, x_to == x)
            dst = dst_of(pl.ds(pl.multiple_of((REACH + phi) * tok + part * x, part), part))

            @pl.when(here)
            def _():
                pltpu.make_async_copy(src.at[:, columns], dst, got.at[REACH + phi]).start()

            @pl.when(jnp.logical_not(here))
            def _():
                pltpu.make_async_remote_copy(
                    src_ref=src.at[:, columns],
                    dst_ref=dst,
                    send_sem=sent,
                    recv_sem=got.at[REACH + phi],
                    device_id=(base + f_to, x_to),
                    device_id_type=MESH,
                ).start()

            return c

        lax.fori_loop(0, 4 * COLS, step, 0)

    def k_at(rows):
        return kbuf.at[rows, :]

    def v_at(rows):
        return vbuf.at[rows, pl.ds(0, DH)]

    def give_mask(j, c):
        f_to = place(x, j)

        @pl.when(f_to == phi)
        def _():
            pltpu.make_async_copy(mine, mbuf.at[REACH + phi], m_got.at[REACH + phi]).start()

        @pl.when(f_to != phi)
        def _():
            pltpu.make_async_remote_copy(
                src_ref=mine,
                dst_ref=mbuf.at[REACH + phi],
                send_sem=m_sent,
                recv_sem=m_got.at[REACH + phi],
                device_id=(base + f_to, x),
                device_id_type=MESH,
            ).start()

        return c

    scatter(qk_ref, k_at, k_sent, k_got)
    lax.fori_loop(0, COLS, give_mask, 0)
    scatter(value_ref, v_at, v_sent, v_got)

    def up(ref_at, got, n, start):
        return pltpu.make_async_remote_copy(
            src_ref=ref_at(rows_of(REACH + PLANE - 1 - n, tok)),
            dst_ref=ref_at(rows_of(REACH - 1 - n, tok)),
            send_sem=halo_sent.at[start + n],
            recv_sem=got.at[REACH - 1 - n],
            device_id=(frame + PLANE, x),
            device_id_type=MESH,
        )

    def down(ref_at, got, n, start):
        return pltpu.make_async_remote_copy(
            src_ref=ref_at(rows_of(REACH + n, tok)),
            dst_ref=ref_at(rows_of(REACH + PLANE + n, tok)),
            send_sem=halo_sent.at[start + n],
            recv_sem=got.at[REACH + PLANE + n],
            device_id=(frame - PLANE, x),
            device_id_type=MESH,
        )

    def mask_up(n):
        return pltpu.make_async_remote_copy(
            src_ref=mbuf.at[REACH + PLANE - 1 - n],
            dst_ref=mbuf.at[REACH - 1 - n],
            send_sem=halo_sent.at[12 + n],
            recv_sem=m_got.at[REACH - 1 - n],
            device_id=(frame + PLANE, x),
            device_id_type=MESH,
        )

    def pass_on(ref_at, got, first):
        for n in range(REACH):
            wait_bytes(ref_at(rows_of(REACH + PLANE - 1 - n, tok)), got.at[REACH + PLANE - 1 - n])

            @pl.when(has_high)
            def _():
                up(ref_at, got, n, first).start()

            wait_bytes(ref_at(rows_of(REACH + n, tok)), got.at[REACH + n])

            @pl.when(has_low)
            def _():
                down(ref_at, got, n, first + REACH).start()

        for n in range(REACH, PLANE - REACH):
            wait_bytes(ref_at(rows_of(REACH + n, tok)), got.at[REACH + n])

    def frame_at(i):
        return jnp.where(i % 2 == 0, PLANE // 2 - 1 - i // 2, PLANE // 2 + i // 2)

    def wait_halo(i, ref_at, got):
        f = frame_at(i)
        low = f < PLANE // 2
        slot = jnp.where(low, f, f + 2 * REACH)

        @pl.when(jnp.logical_and(i >= 2, jnp.where(low, has_low, has_high)))
        def _():
            wait_bytes(ref_at(rows_of(slot, tok)), got.at[slot])

    def weigh(f):
        q = kbuf[rows_of(f + REACH, tok), :]
        bias = []
        for g in range(SPAN):
            k = g - REACH
            if k < 0:
                bias.append(mbuf[REACH + f + k, pl.ds(-k - 1, 1), :])
            elif k == 0:
                bias.append(None)
            else:
                listed = mbuf[REACH + f, pl.ds(k - 1, 1), :]
                bias.append(jnp.where(jnp.logical_or(has_high, f + k < PLANE), listed, DEAD))
        best = None
        for g in range(SPAN):
            k = kbuf[rows_of(f + g, tok), :]
            s = lax.dot_general(q, k, (((1,), (1,)), ((), ())), preferred_element_type=jnp.float32)
            if g == REACH:
                first = lax.broadcasted_iota(jnp.int32, s.shape, 0)
                second = lax.broadcasted_iota(jnp.int32, s.shape, 1)
                s = jnp.where(first == second, -DEAD, s)
            sbuf[:, g * tok : (g + 1) * tok] = s
            t = functools.reduce(jnp.maximum, [s[:, c : c + DH] for c in range(0, tok, DH)])
            if g != REACH:
                t = t - bias[g]
            best = t if best is None else jnp.maximum(best, t)
        best = jnp.broadcast_to(jnp.max(best, axis=1, keepdims=True) * LOG2, (tok, DH))
        for g in range(SPAN):
            less = best if g == REACH else best + bias[g]
            for c in range(g * tok, (g + 1) * tok, DH):
                pbuf[f, :, c : c + DH] = jnp.exp2(sbuf[:, c : c + DH] * LOG2 - less).astype(jnp.bfloat16)

    def give_out(f, x_to, here):
        rows = pl.ds(pl.multiple_of(f * tok, tok) + x_to * part, part)
        columns = pl.ds(pl.multiple_of(head * DH, DH), DH)

        @pl.when(here)
        def _():
            pltpu.make_async_copy(obuf.at[rows, :], out_ref.at[:, columns], o_got).start()

        @pl.when(jnp.logical_not(here))
        def _():
            pltpu.make_async_remote_copy(
                src_ref=obuf.at[rows, :],
                dst_ref=out_ref.at[:, columns],
                send_sem=o_sent,
                recv_sem=o_got,
                device_id=(base + f, x_to),
                device_id_type=MESH,
            ).start()

    @pl.when(active)
    def _():
        pass_on(k_at, k_got, 0)
        for n in range(PLANE):
            wait_bytes(mbuf.at[REACH + n], m_got.at[REACH + n])
        for n in range(REACH):

            @pl.when(has_high)
            def _():
                mask_up(n).start()

        @pl.when(has_low)
        def _():
            for n in range(REACH):
                wait_bytes(mbuf.at[n], m_got.at[n])

        def scores_step(i, c):
            wait_halo(i, k_at, k_got)
            weigh(frame_at(i))

            @pl.when(i == 4)
            def _():
                pass_on(v_at, v_got, 6)

            return c

        lax.fori_loop(0, PLANE, scores_step, 0)

        def value_step(i, c):
            wait_halo(i, v_at, v_got)
            f = frame_at(i)
            values = vbuf[pl.ds(pl.multiple_of(f * tok, tok), SPAN * tok), :]
            o = jnp.dot(pbuf[f], values, preferred_element_type=jnp.float32)
            obuf[rows_of(f, tok), :] = (o[:, :DH] / o[:, DH:]).astype(jnp.bfloat16)
            for x_to in range(4):
                give_out(f, x_to, jnp.logical_and(f == phi, x == x_to))
            return c

        lax.fori_loop(0, PLANE, value_step, 0)

        wait_bytes(qk_ref.at[:, pl.ds(0, (4 * COLS - 1) * DH)], k_sent)
        wait_bytes(value_ref.at[:, pl.ds(0, (4 * COLS - 1) * DH)], v_sent)
        wait_bytes(mbuf.at[pl.ds(0, COLS - 1)], m_sent)
        wait_bytes(obuf.at[pl.ds(0, (4 * PLANE - 1) * part), :], o_sent)

        @pl.when(has_high)
        def _():
            for n in range(REACH):
                up(k_at, k_got, n, 0).wait_send()
                up(v_at, v_got, n, 6).wait_send()
                mask_up(n).wait_send()

        @pl.when(has_low)
        def _():
            for n in range(REACH):
                down(k_at, k_got, n, REACH).wait_send()
                down(v_at, v_got, n, 6 + REACH).wait_send()

    @pl.when(jnp.logical_not(active))
    def _():
        wait_bytes(qk_ref, k_sent)
        wait_bytes(value_ref, v_sent)
        wait_bytes(mbuf.at[pl.ds(0, COLS)], m_sent)

    wait_bytes(out_ref, o_got)


def solution(mesh):
    planes = mesh.shape["frame"] // PLANE

    def local(qk, value, pair_mask):
        part, width = qk.shape
        tok = 4 * part
        return pl.pallas_call(
            functools.partial(kernel, planes),
            out_shape=jax.ShapeDtypeStruct((part, width), jnp.bfloat16),
            in_specs=[
                pl.BlockSpec(memory_space=pl.ANY),
                pl.BlockSpec(memory_space=pl.ANY),
                pl.BlockSpec(memory_space=pltpu.SMEM),
            ],
            out_specs=pl.BlockSpec(memory_space=pl.ANY),
            scratch_shapes=[
                pltpu.VMEM((SLOTS * tok, DH), jnp.bfloat16),
                pltpu.VMEM((SLOTS * tok, 2 * DH), jnp.bfloat16),
                pltpu.VMEM((PLANE + REACH, 8, DH), jnp.float32),
                pltpu.VMEM((8, DH), jnp.float32),
                pltpu.VMEM((PLANE, tok, SPAN * tok), jnp.bfloat16),
                pltpu.VMEM((tok, SPAN * tok), jnp.float32),
                pltpu.VMEM((PLANE * tok, DH), jnp.bfloat16),
                pltpu.SemaphoreType.DMA,
                pltpu.SemaphoreType.DMA,
                pltpu.SemaphoreType.DMA,
                pltpu.SemaphoreType.DMA,
                pltpu.SemaphoreType.DMA((15,)),
                pltpu.SemaphoreType.DMA((SLOTS,)),
                pltpu.SemaphoreType.DMA((SLOTS,)),
                pltpu.SemaphoreType.DMA((PLANE + REACH,)),
                pltpu.SemaphoreType.DMA,
            ],
            compiler_params=pltpu.CompilerParams(
                collective_id=0, has_side_effects=True, vmem_limit_bytes=52 * 2**20
            ),
        )(qk, value, pair_mask)

    return jax.shard_map(
        local,
        mesh=mesh,
        in_specs=(P(("frame", "head"), None), P(("frame", "head"), None), P("frame", None)),
        out_specs=P(("frame", "head"), None),
        check_vma=False,
    )
```

```python
import functools
import math

import jax
import jax.numpy as jnp
from jax import lax
from jax.experimental import pallas as pl
from jax.experimental.pallas import tpu as pltpu
from jax.sharding import PartitionSpec as P

MESH = pl.DeviceIdType.MESH
DH = 128
PLANE = 8
REACH = 3
SPAN = 2 * REACH + 1
SLOTS = PLANE + 2 * REACH
COLS = 6
DEAD = 1e30
V_STEP = 5
LOG2 = math.log2(math.e) / math.sqrt(DH)


def rows_of(slot, tok):
    return pl.ds(pl.multiple_of(slot * tok, tok), tok)


def wait_bytes(ref, sem):
    pltpu.make_async_copy(ref, ref, sem).wait()


def kernel(
    planes,
    qk_ref,
    value_ref,
    mask_ref,
    out_ref,
    kbuf,
    vbuf,
    mbuf,
    mine,
    listed,
    pbuf,
    sbuf,
    obuf,
    k_sent,
    v_sent,
    m_sent,
    o_sent,
    up_sent,
    down_sent,
    k_got,
    v_got,
    k_halo,
    v_halo,
    m_got,
    o_got,
    listed_got,
):
    part = qk_ref.shape[0]
    tok = 4 * part
    frame, x = lax.axis_index("frame"), lax.axis_index("head")
    z, phi = frame // PLANE, frame % PLANE
    base = frame - phi
    own_shift = 2 * (x % 2)
    seat = (phi - own_shift + PLANE) % PLANE
    active = seat % 4 != 3
    head = COLS * x + seat - seat // 4
    has_low, has_high = z > 0, z < planes - 1

    def place(x_to, j):
        return (j + j // 3 + 2 * (x_to % 2)) % PLANE

    row_copy = pltpu.make_async_copy(mask_ref, listed, listed_got)
    row_copy.start()

    barrier = pltpu.get_barrier_semaphore()

    def greet(i, c):
        f_to, x_to = i // 4, i % 4

        @pl.when(jnp.logical_or(f_to != phi, x_to != x))
        def _():
            pl.semaphore_signal(barrier, 1, device_id=(base + f_to, x_to), device_id_type=MESH)

        return c

    lax.fori_loop(0, 4 * PLANE, greet, 0)

    @pl.when(has_low)
    def _():
        pl.semaphore_signal(barrier, 1, device_id=(frame - PLANE, x), device_id_type=MESH)

    @pl.when(has_high)
    def _():
        pl.semaphore_signal(barrier, 1, device_id=(frame + PLANE, x), device_id_type=MESH)

    row_copy.wait()
    row = lax.broadcasted_iota(jnp.int32, mine.shape, 0)
    picked = jnp.where(row == 0, listed[0, 0], jnp.where(row == 1, listed[0, 1], listed[0, 2]))
    mine[...] = jnp.where(picked == 1, 0.0, DEAD).astype(jnp.float32)
    vbuf[:, DH:] = jnp.ones((SLOTS * tok, DH), jnp.bfloat16)

    @pl.when(jnp.logical_not(has_low))
    def _():
        kbuf[: REACH * tok, :] = jnp.zeros((REACH * tok, DH), jnp.bfloat16)
        vbuf[: REACH * tok, :DH] = jnp.zeros((REACH * tok, DH), jnp.bfloat16)
        for s in range(REACH):
            mbuf[s] = jnp.full(mine.shape, DEAD, jnp.float32)

    @pl.when(jnp.logical_not(has_high))
    def _():
        kbuf[(PLANE + REACH) * tok :, :] = jnp.zeros((REACH * tok, DH), jnp.bfloat16)
        vbuf[(PLANE + REACH) * tok :, :DH] = jnp.zeros((REACH * tok, DH), jnp.bfloat16)

    greeted = 4 * PLANE - 1 + has_low.astype(jnp.int32) + has_high.astype(jnp.int32)
    pl.semaphore_wait(barrier, greeted)

    def offset(i):
        q, dx = i // 4, i % 4
        return dx, (q + dx) % 4, (q // 4 + dx) % 2

    def target(i):
        dx, dy, dc = offset(i)
        x_to = (x + dx) % 4
        f_to = (phi // 2 + dy) % 4 * 2 + (phi + dc) % 2
        seat_to = (f_to + 2 * PLANE - 2 * (x_to % 2)) % PLANE
        return x_to, f_to, seat_to % 4 != 3, COLS * x_to + seat_to - seat_to // 4

    def origin(i):
        dx, dy, dc = offset(i)
        return (x + 4 - dx) % 4, (phi // 2 + 4 - dy) % 4 * 2 + (phi + dc) % 2

    def chunk(f, x_of):
        return pl.ds(pl.multiple_of((REACH + f) * tok + part * x_of, part), part)

    def parcel(i, src, dst_at, sent, got):
        x_to, f_to, _, head_to = target(i)
        return pltpu.make_async_remote_copy(
            src_ref=src.at[:, pl.ds(pl.multiple_of(head_to * DH, DH), DH)],
            dst_ref=dst_at(chunk(phi, x)),
            send_sem=sent,
            recv_sem=got.at[i],
            device_id=(base + f_to, x_to),
            device_id_type=MESH,
        )

    def keep(src, dst_at, got):
        columns = pl.ds(pl.multiple_of(head * DH, DH), DH)
        pltpu.make_async_copy(src.at[:, columns], dst_at(chunk(phi, x)), got.at[0]).start()

    def k_at(rows):
        return kbuf.at[rows, :]

    def v_at(rows):
        return vbuf.at[rows, pl.ds(0, DH)]

    def give_mask(j, c):
        f_to = place(x, j)

        @pl.when(f_to == phi)
        def _():
            pltpu.make_async_copy(mine, mbuf.at[REACH + phi], m_got.at[REACH + phi]).start()

        @pl.when(f_to != phi)
        def _():
            pltpu.make_async_remote_copy(
                src_ref=mine,
                dst_ref=mbuf.at[REACH + phi],
                send_sem=m_sent,
                recv_sem=m_got.at[REACH + phi],
                device_id=(base + f_to, x),
                device_id_type=MESH,
            ).start()

        return c

    def qk_parcel(i):
        return parcel(i, qk_ref, k_at, k_sent.at[i], k_got)

    def value_parcel(i):
        return parcel(i, value_ref, v_at, v_sent, v_got)

    def send_qk(i, c):
        @pl.when(target(i)[2])
        def _():
            qk_parcel(i).start()

        return c

    def pass_on(i, ref_at, got, halo, kind):
        x_of, f = origin(i)
        here = ref_at(chunk(f, x_of))
        wait_bytes(here, got.at[i])

        @pl.when(jnp.logical_and(f >= PLANE - REACH, has_high))
        def _():
            pltpu.make_async_remote_copy(
                src_ref=here,
                dst_ref=ref_at(chunk(f - PLANE, x_of)),
                send_sem=up_sent.at[kind],
                recv_sem=halo.at[f - PLANE + REACH],
                device_id=(frame + PLANE, x),
                device_id_type=MESH,
            ).start()

        @pl.when(jnp.logical_and(f < REACH, has_low))
        def _():
            pltpu.make_async_remote_copy(
                src_ref=here,
                dst_ref=ref_at(chunk(f + PLANE, x_of)),
                send_sem=down_sent.at[kind],
                recv_sem=halo.at[f + REACH],
                device_id=(frame - PLANE, x),
                device_id_type=MESH,
            ).start()

    def exchange(i, c):
        @pl.when(jnp.logical_and(target(i)[2], i > 0))
        def _():
            qk_parcel(i).wait_send()
            value_parcel(i).start()

        @pl.when(active)
        def _():
            pass_on(i, k_at, k_got, k_halo, 0)

        return c

    lax.fori_loop(0, COLS, give_mask, 0)
    lax.fori_loop(1, 4 * PLANE, send_qk, 0)

    @pl.when(active)
    def _():
        keep(qk_ref, k_at, k_got)
        keep(value_ref, v_at, v_got)

    def mask_up(n):
        return pltpu.make_async_remote_copy(
            src_ref=mbuf.at[REACH + PLANE - 1 - n],
            dst_ref=mbuf.at[REACH - 1 - n],
            send_sem=up_sent.at[2 + n],
            recv_sem=m_got.at[REACH - 1 - n],
            device_id=(frame + PLANE, x),
            device_id_type=MESH,
        )

    def frame_at(i):
        return jnp.where((i + x) % 2 == 0, PLANE // 2 - 1 - i // 2, PLANE // 2 + i // 2)

    def wait_halo(f, ref_at, halo):
        low = f < PLANE // 2
        slot = jnp.where(low, f, f + 2 * REACH)
        index = jnp.where(low, f, f - PLANE + 2 * REACH)

        @pl.when(jnp.where(low, has_low, has_high))
        def _():
            wait_bytes(ref_at(rows_of(slot, tok)), halo.at[index])

    def weigh(f):
        q = kbuf[rows_of(f + REACH, tok), :]
        bias = []
        for g in range(SPAN):
            k = g - REACH
            if k < 0:
                bias.append(mbuf[REACH + f + k, pl.ds(-k - 1, 1), :])
            elif k == 0:
                bias.append(None)
            else:
                given = mbuf[REACH + f, pl.ds(k - 1, 1), :]
                bias.append(jnp.where(jnp.logical_or(has_high, f + k < PLANE), given, DEAD))
        best = None
        for g in range(SPAN):
            k = kbuf[rows_of(f + g, tok), :]
            s = lax.dot_general(q, k, (((1,), (1,)), ((), ())), preferred_element_type=jnp.float32)
            if g == REACH:
                first = lax.broadcasted_iota(jnp.int32, s.shape, 0)
                second = lax.broadcasted_iota(jnp.int32, s.shape, 1)
                s = jnp.where(first == second, -DEAD, s)
            sbuf[:, g * tok : (g + 1) * tok] = s
            t = functools.reduce(jnp.maximum, [s[:, c : c + DH] for c in range(0, tok, DH)])
            if g != REACH:
                t = t - bias[g]
            best = t if best is None else jnp.maximum(best, t)
        best = jnp.broadcast_to(jnp.max(best, axis=1, keepdims=True) * LOG2, (tok, DH))
        for g in range(SPAN):
            less = best if g == REACH else best + bias[g]
            for c in range(g * tok, (g + 1) * tok, DH):
                pbuf[f, :, c : c + DH] = jnp.exp2(sbuf[:, c : c + DH] * LOG2 - less).astype(jnp.bfloat16)

    def give_out(f, x_to, here):
        rows = pl.ds(pl.multiple_of(f * tok, tok) + x_to * part, part)
        columns = pl.ds(pl.multiple_of(head * DH, DH), DH)

        @pl.when(here)
        def _():
            pltpu.make_async_copy(obuf.at[rows, :], out_ref.at[:, columns], o_got).start()

        @pl.when(jnp.logical_not(here))
        def _():
            pltpu.make_async_remote_copy(
                src_ref=obuf.at[rows, :],
                dst_ref=out_ref.at[:, columns],
                send_sem=o_sent,
                recv_sem=o_got,
                device_id=(base + f, x_to),
                device_id_type=MESH,
            ).start()

    lax.fori_loop(0, PLANE, exchange, 0)

    @pl.when(active)
    def _():
        for n in range(PLANE):
            wait_bytes(mbuf.at[REACH + n], m_got.at[REACH + n])
        for n in range(REACH):

            @pl.when(has_high)
            def _():
                mask_up(n).start()

    lax.fori_loop(PLANE, 4 * PLANE, exchange, 0)

    @pl.when(active)
    def _():
        def scores_step(i, c):
            f = frame_at(i)

            @pl.when(i >= 2)
            def _():
                wait_halo(f, k_at, k_halo)

            @pl.when(jnp.logical_and(i == 2, has_low))
            def _():
                for n in range(REACH):
                    wait_bytes(mbuf.at[n], m_got.at[n])

            weigh(f)

            def hand_on(n, c):
                pass_on(n, v_at, v_got, v_halo, 1)
                return c

            lax.fori_loop(V_STEP * i, jnp.minimum(V_STEP * (i + 1), 4 * PLANE), hand_on, 0)
            return c

        lax.fori_loop(0, PLANE, scores_step, 0)

        def value_step(i, c):
            f = frame_at(i)

            @pl.when(i >= 2)
            def _():
                wait_halo(f, v_at, v_halo)

            values = vbuf[pl.ds(pl.multiple_of(f * tok, tok), SPAN * tok), :]
            o = jnp.dot(pbuf[f], values, preferred_element_type=jnp.float32)
            obuf[rows_of(f, tok), :] = (o[:, :DH] / o[:, DH:]).astype(jnp.bfloat16)
            for x_to in range(4):
                give_out(f, x_to, jnp.logical_and(f == phi, x == x_to))
            return c

        lax.fori_loop(0, PLANE, value_step, 0)

        wait_bytes(value_ref.at[:, pl.ds(0, (4 * COLS - 1) * DH)], v_sent)
        wait_bytes(mbuf.at[pl.ds(0, COLS - 1)], m_sent)
        wait_bytes(obuf.at[pl.ds(0, (4 * PLANE - 1) * part), :], o_sent)

        @pl.when(has_high)
        def _():
            wait_bytes(kbuf.at[pl.ds(0, REACH * tok), :], up_sent.at[0])
            wait_bytes(v_at(pl.ds(0, REACH * tok)), up_sent.at[1])
            for n in range(REACH):
                mask_up(n).wait_send()

        @pl.when(has_low)
        def _():
            wait_bytes(kbuf.at[pl.ds(0, REACH * tok), :], down_sent.at[0])
            wait_bytes(v_at(pl.ds(0, REACH * tok)), down_sent.at[1])

    @pl.when(jnp.logical_not(active))
    def _():
        wait_bytes(value_ref, v_sent)
        wait_bytes(mbuf.at[pl.ds(0, COLS)], m_sent)

    wait_bytes(out_ref, o_got)


def solution(mesh):
    planes = mesh.shape["frame"] // PLANE

    def local(qk, value, pair_mask):
        part, width = qk.shape
        tok = 4 * part
        return pl.pallas_call(
            functools.partial(kernel, planes),
            out_shape=jax.ShapeDtypeStruct((part, width), jnp.bfloat16),
            in_specs=[
                pl.BlockSpec(memory_space=pl.ANY),
                pl.BlockSpec(memory_space=pl.ANY),
                pl.BlockSpec(memory_space=pl.ANY),
            ],
            out_specs=pl.BlockSpec(memory_space=pl.ANY),
            scratch_shapes=[
                pltpu.VMEM((SLOTS * tok, DH), jnp.bfloat16),
                pltpu.VMEM((SLOTS * tok, 2 * DH), jnp.bfloat16),
                pltpu.VMEM((PLANE + REACH, 8, DH), jnp.float32),
                pltpu.VMEM((8, DH), jnp.float32),
                pltpu.SMEM((1, REACH), jnp.int32),
                pltpu.VMEM((PLANE, tok, SPAN * tok), jnp.bfloat16),
                pltpu.VMEM((tok, SPAN * tok), jnp.float32),
                pltpu.VMEM((PLANE * tok, DH), jnp.bfloat16),
                pltpu.SemaphoreType.DMA((4 * PLANE,)),
                pltpu.SemaphoreType.DMA,
                pltpu.SemaphoreType.DMA,
                pltpu.SemaphoreType.DMA,
                pltpu.SemaphoreType.DMA((2 + REACH,)),
                pltpu.SemaphoreType.DMA((2,)),
                pltpu.SemaphoreType.DMA((4 * PLANE,)),
                pltpu.SemaphoreType.DMA((4 * PLANE,)),
                pltpu.SemaphoreType.DMA((2 * REACH,)),
                pltpu.SemaphoreType.DMA((2 * REACH,)),
                pltpu.SemaphoreType.DMA((PLANE + REACH,)),
                pltpu.SemaphoreType.DMA,
                pltpu.SemaphoreType.DMA,
            ],
            compiler_params=pltpu.CompilerParams(
                collective_id=0, has_side_effects=True, vmem_limit_bytes=63 * 2**20
            ),
        )(qk, value, pair_mask)

    return jax.shard_map(
        local,
        mesh=mesh,
        in_specs=(P(("frame", "head"), None), P(("frame", "head"), None), P("frame", None)),
        out_specs=P(("frame", "head"), None),
        check_vma=False,
    )
```

```python
import functools
import math

import jax
import jax.numpy as jnp
from jax import lax
from jax.experimental import pallas as pl
from jax.experimental.pallas import tpu as pltpu
from jax.sharding import PartitionSpec as P

MESH = pl.DeviceIdType.MESH
DH = 128
PLANE = 8
REACH = 3
SPAN = 2 * REACH + 1
SLOTS = PLANE + 2 * REACH
COLS = 6
DEAD = 1e30
LATE = 2
PIECES = 3
V_STEP = 11
LOG2 = math.log2(math.e) / math.sqrt(DH)


def rows_of(slot, tok):
    return pl.ds(pl.multiple_of(slot * tok, tok), tok)


def wait_bytes(ref, sem):
    pltpu.make_async_copy(ref, ref, sem).wait()


def kernel(
    planes,
    qk_ref,
    value_ref,
    mask_ref,
    out_ref,
    kbuf,
    vbuf,
    mbuf,
    mine,
    listed,
    pbuf,
    sbuf,
    obuf,
    k_sent,
    v_sent,
    m_sent,
    o_sent,
    up_sent,
    down_sent,
    k_got,
    v_got,
    k_halo,
    v_halo,
    m_got,
    o_got,
    listed_got,
):
    part = qk_ref.shape[0]
    tok = 4 * part
    frame, x = lax.axis_index("frame"), lax.axis_index("head")
    z, phi = frame // PLANE, frame % PLANE
    base = frame - phi
    own_shift = 2 * (x % 2)
    seat = (phi - own_shift + PLANE) % PLANE
    active = seat % 4 != 3
    head = COLS * x + seat - seat // 4
    has_low, has_high = z > 0, z < planes - 1

    def place(x_to, j):
        return (j + j // 3 + 2 * (x_to % 2)) % PLANE

    row_copy = pltpu.make_async_copy(mask_ref, listed, listed_got)
    row_copy.start()

    barrier = pltpu.get_barrier_semaphore()

    def greet(i, c):
        f_to, x_to = i // 4, i % 4

        @pl.when(jnp.logical_or(f_to != phi, x_to != x))
        def _():
            pl.semaphore_signal(barrier, 1, device_id=(base + f_to, x_to), device_id_type=MESH)

        return c

    lax.fori_loop(0, 4 * PLANE, greet, 0)

    @pl.when(has_low)
    def _():
        pl.semaphore_signal(barrier, 1, device_id=(frame - PLANE, x), device_id_type=MESH)

    @pl.when(has_high)
    def _():
        pl.semaphore_signal(barrier, 1, device_id=(frame + PLANE, x), device_id_type=MESH)

    row_copy.wait()
    row = lax.broadcasted_iota(jnp.int32, mine.shape, 0)
    picked = jnp.where(row == 0, listed[0, 0], jnp.where(row == 1, listed[0, 1], listed[0, 2]))
    mine[...] = jnp.where(picked == 1, 0.0, DEAD).astype(jnp.float32)
    vbuf[:, DH:] = jnp.ones((SLOTS * tok, DH), jnp.bfloat16)

    @pl.when(jnp.logical_not(has_low))
    def _():
        kbuf[: REACH * tok, :] = jnp.zeros((REACH * tok, DH), jnp.bfloat16)
        vbuf[: REACH * tok, :DH] = jnp.zeros((REACH * tok, DH), jnp.bfloat16)
        for s in range(REACH):
            mbuf[s] = jnp.full(mine.shape, DEAD, jnp.float32)

    @pl.when(jnp.logical_not(has_high))
    def _():
        kbuf[(PLANE + REACH) * tok :, :] = jnp.zeros((REACH * tok, DH), jnp.bfloat16)
        vbuf[(PLANE + REACH) * tok :, :DH] = jnp.zeros((REACH * tok, DH), jnp.bfloat16)

    greeted = 4 * PLANE - 1 + has_low.astype(jnp.int32) + has_high.astype(jnp.int32)
    pl.semaphore_wait(barrier, greeted)

    def offset(i):
        q, dx = i // 4, i % 4
        return dx, (q + dx) % 4, (q // 4 + dx) % 2

    def target(i):
        dx, dy, dc = offset(i)
        x_to = (x + dx) % 4
        f_to = (phi // 2 + dy) % 4 * 2 + (phi + dc) % 2
        seat_to = (f_to + 2 * PLANE - 2 * (x_to % 2)) % PLANE
        return x_to, f_to, seat_to % 4 != 3, COLS * x_to + seat_to - seat_to // 4

    def origin(i):
        dx, dy, dc = offset(i)
        return (x + 4 - dx) % 4, (phi // 2 + 4 - dy) % 4 * 2 + (phi + dc) % 2

    def chunk(f, x_of):
        return pl.ds(pl.multiple_of((REACH + f) * tok + part * x_of, part), part)

    def parcel(i, src, dst_at, sent, got):
        x_to, f_to, _, head_to = target(i)
        return pltpu.make_async_remote_copy(
            src_ref=src.at[:, pl.ds(pl.multiple_of(head_to * DH, DH), DH)],
            dst_ref=dst_at(chunk(phi, x)),
            send_sem=sent,
            recv_sem=got.at[i],
            device_id=(base + f_to, x_to),
            device_id_type=MESH,
        )

    def keep(src, dst_at, got):
        columns = pl.ds(pl.multiple_of(head * DH, DH), DH)
        pltpu.make_async_copy(src.at[:, columns], dst_at(chunk(phi, x)), got.at[0]).start()

    def k_at(rows):
        return kbuf.at[rows, :]

    def v_at(rows):
        return vbuf.at[rows, pl.ds(0, DH)]

    def give_mask(j, c):
        f_to = place(x, j)

        @pl.when(f_to == phi)
        def _():
            pltpu.make_async_copy(mine, mbuf.at[REACH + phi], m_got.at[REACH + phi]).start()

        @pl.when(f_to != phi)
        def _():
            pltpu.make_async_remote_copy(
                src_ref=mine,
                dst_ref=mbuf.at[REACH + phi],
                send_sem=m_sent,
                recv_sem=m_got.at[REACH + phi],
                device_id=(base + f_to, x),
                device_id_type=MESH,
            ).start()

        return c

    def qk_parcel(i):
        return parcel(i, qk_ref, k_at, k_sent.at[i], k_got)

    def value_parcel(i):
        return parcel(i, value_ref, v_at, v_sent, v_got)

    def send_qk(i, c):
        @pl.when(target(i)[2])
        def _():
            qk_parcel(i).start()

        return c

    def pass_on(i, ref_at, got, halo, kind):
        x_of, f = origin(i)
        here = ref_at(chunk(f, x_of))
        wait_bytes(here, got.at[i])

        @pl.when(jnp.logical_and(f >= PLANE - REACH, has_high))
        def _():
            pltpu.make_async_remote_copy(
                src_ref=here,
                dst_ref=ref_at(chunk(f - PLANE, x_of)),
                send_sem=up_sent.at[kind],
                recv_sem=halo.at[f - PLANE + REACH],
                device_id=(frame + PLANE, x),
                device_id_type=MESH,
            ).start()

        @pl.when(jnp.logical_and(f < REACH, has_low))
        def _():
            pltpu.make_async_remote_copy(
                src_ref=here,
                dst_ref=ref_at(chunk(f + PLANE, x_of)),
                send_sem=down_sent.at[kind],
                recv_sem=halo.at[f + REACH],
                device_id=(frame - PLANE, x),
                device_id_type=MESH,
            ).start()

    def exchange(i, c):
        @pl.when(jnp.logical_and(target(i)[2], i > 0))
        def _():
            qk_parcel(i).wait_send()
            value_parcel(i).start()

        @pl.when(active)
        def _():
            pass_on(i, k_at, k_got, k_halo, 0)

        return c

    lax.fori_loop(0, COLS, give_mask, 0)
    lax.fori_loop(1, 4 * PLANE, send_qk, 0)

    @pl.when(active)
    def _():
        keep(qk_ref, k_at, k_got)
        keep(value_ref, v_at, v_got)

    def mask_up(n):
        return pltpu.make_async_remote_copy(
            src_ref=mbuf.at[REACH + PLANE - 1 - n],
            dst_ref=mbuf.at[REACH - 1 - n],
            send_sem=up_sent.at[2 + n],
            recv_sem=m_got.at[REACH - 1 - n],
            device_id=(frame + PLANE, x),
            device_id_type=MESH,
        )

    def frame_at(i):
        return jnp.where((i + x) % 2 == 0, PLANE // 2 - 1 - i // 2, PLANE // 2 + i // 2)

    def wait_halo(f, ref_at, halo):
        low = f < PLANE // 2
        slot = jnp.where(low, f, f + 2 * REACH)
        index = jnp.where(low, f, f - PLANE + 2 * REACH)

        @pl.when(jnp.where(low, has_low, has_high))
        def _():
            wait_bytes(ref_at(rows_of(slot, tok)), halo.at[index])

    def weigh(f):
        q = kbuf[rows_of(f + REACH, tok), :]
        bias = []
        for g in range(SPAN):
            k = g - REACH
            if k < 0:
                bias.append(mbuf[REACH + f + k, pl.ds(-k - 1, 1), :])
            elif k == 0:
                bias.append(None)
            else:
                given = mbuf[REACH + f, pl.ds(k - 1, 1), :]
                bias.append(jnp.where(jnp.logical_or(has_high, f + k < PLANE), given, DEAD))
        best = None
        for g in range(SPAN):
            k = kbuf[rows_of(f + g, tok), :]
            s = lax.dot_general(q, k, (((1,), (1,)), ((), ())), preferred_element_type=jnp.float32)
            if g == REACH:
                first = lax.broadcasted_iota(jnp.int32, s.shape, 0)
                second = lax.broadcasted_iota(jnp.int32, s.shape, 1)
                s = jnp.where(first == second, -DEAD, s)
            sbuf[:, g * tok : (g + 1) * tok] = s
            t = functools.reduce(jnp.maximum, [s[:, c : c + DH] for c in range(0, tok, DH)])
            if g != REACH:
                t = t - bias[g]
            best = t if best is None else jnp.maximum(best, t)
        best = jnp.broadcast_to(jnp.max(best, axis=1, keepdims=True) * LOG2, (tok, DH))
        for g in range(SPAN):
            less = best if g == REACH else best + bias[g]
            for c in range(g * tok, (g + 1) * tok, DH):
                pbuf[f, :, c : c + DH] = jnp.exp2(sbuf[:, c : c + DH] * LOG2 - less).astype(jnp.bfloat16)

    def give_out(f, x_to, here):
        rows = pl.ds(pl.multiple_of(f * tok, tok) + x_to * part, part)
        columns = pl.ds(pl.multiple_of(head * DH, DH), DH)

        @pl.when(here)
        def _():
            pltpu.make_async_copy(obuf.at[rows, :], out_ref.at[:, columns], o_got).start()

        @pl.when(jnp.logical_not(here))
        def _():
            pltpu.make_async_remote_copy(
                src_ref=obuf.at[rows, :],
                dst_ref=out_ref.at[:, columns],
                send_sem=o_sent,
                recv_sem=o_got,
                device_id=(base + f, x_to),
                device_id_type=MESH,
            ).start()

    lax.fori_loop(0, PLANE, exchange, 0)

    @pl.when(active)
    def _():
        for n in range(PLANE):
            wait_bytes(mbuf.at[REACH + n], m_got.at[REACH + n])
        for n in range(REACH):

            @pl.when(has_high)
            def _():
                mask_up(n).start()

    lax.fori_loop(PLANE, 4 * PLANE, exchange, 0)

    @pl.when(active)
    def _():
        def scores_step(i, c):
            f = frame_at(i)

            @pl.when(i >= 2)
            def _():
                wait_halo(f, k_at, k_halo)

            @pl.when(jnp.logical_and(i == 2, has_low))
            def _():
                for n in range(REACH):
                    wait_bytes(mbuf.at[n], m_got.at[n])

            weigh(f)

            def hand_on(n, c):
                pass_on(n, v_at, v_got, v_halo, 1)
                return c

            lax.fori_loop(V_STEP * i, jnp.minimum(V_STEP * (i + 1), 4 * PLANE), hand_on, 0)
            return c

        lax.fori_loop(0, PLANE, scores_step, 0)

        def value_step(i, c):
            rest = PLANE - LATE
            f = frame_at(jnp.where(i < LATE, i, LATE + (i - LATE + 2 * ((phi // 2 + x) % 3)) % rest))

            @pl.when(i == LATE)
            def _():
                for n in range(LATE, PLANE):
                    wait_halo(frame_at(n), v_at, v_halo)

            values = vbuf[pl.ds(pl.multiple_of(f * tok, tok), SPAN * tok), :]
            o = jnp.dot(pbuf[f], values, preferred_element_type=jnp.float32)
            obuf[rows_of(f, tok), :] = (o[:, :DH] / o[:, DH:]).astype(jnp.bfloat16)
            for x_to in range(4):
                give_out(f, x_to, jnp.logical_and(f == phi, x == x_to))
            return c

        lax.fori_loop(0, PLANE, value_step, 0)

        wait_bytes(value_ref.at[:, pl.ds(0, (4 * COLS - 1) * DH)], v_sent)
        wait_bytes(mbuf.at[pl.ds(0, COLS - 1)], m_sent)
        wait_bytes(obuf.at[pl.ds(0, (4 * PLANE - 1) * part), :], o_sent)

        @pl.when(has_high)
        def _():
            wait_bytes(kbuf.at[pl.ds(0, REACH * tok), :], up_sent.at[0])
            wait_bytes(v_at(pl.ds(0, REACH * tok)), up_sent.at[1])
            for n in range(REACH):
                mask_up(n).wait_send()

        @pl.when(has_low)
        def _():
            wait_bytes(kbuf.at[pl.ds(0, REACH * tok), :], down_sent.at[0])
            wait_bytes(v_at(pl.ds(0, REACH * tok)), down_sent.at[1])

    @pl.when(jnp.logical_not(active))
    def _():
        wait_bytes(value_ref, v_sent)
        wait_bytes(mbuf.at[pl.ds(0, COLS)], m_sent)

    wait_bytes(out_ref, o_got)


def hand_over(src, dst, buffer, came, went):
    step = src.shape[0] // PIECES
    into, out = [], []
    for n in range(PIECES):
        rows = pl.ds(n * step, step)
        into.append(pltpu.make_async_copy(src.at[rows, :], buffer.at[rows, :], came.at[n]))
        out.append(pltpu.make_async_copy(buffer.at[rows, :], dst.at[rows, :], went.at[n]))
    for copy in into:
        copy.start()
    for first, second in zip(into, out):
        first.wait()
        second.start()
    for copy in out:
        copy.wait()


def solution(mesh):
    planes = mesh.shape["frame"] // PLANE

    def local(qk, value, pair_mask):
        part, width = qk.shape
        tok = 4 * part
        made = pl.pallas_call(
            functools.partial(kernel, planes),
            out_shape=jax.ShapeDtypeStruct((part, width), jnp.bfloat16),
            in_specs=[
                pl.BlockSpec(memory_space=pl.ANY),
                pl.BlockSpec(memory_space=pl.ANY),
                pl.BlockSpec(memory_space=pl.ANY),
            ],
            out_specs=pl.BlockSpec(memory_space=pl.ANY),
            scratch_shapes=[
                pltpu.VMEM((SLOTS * tok, DH), jnp.bfloat16),
                pltpu.VMEM((SLOTS * tok, 2 * DH), jnp.bfloat16),
                pltpu.VMEM((PLANE + REACH, 8, DH), jnp.float32),
                pltpu.VMEM((8, DH), jnp.float32),
                pltpu.SMEM((1, REACH), jnp.int32),
                pltpu.VMEM((PLANE, tok, SPAN * tok), jnp.bfloat16),
                pltpu.VMEM((tok, SPAN * tok), jnp.float32),
                pltpu.VMEM((PLANE * tok, DH), jnp.bfloat16),
                pltpu.SemaphoreType.DMA((4 * PLANE,)),
                pltpu.SemaphoreType.DMA,
                pltpu.SemaphoreType.DMA,
                pltpu.SemaphoreType.DMA,
                pltpu.SemaphoreType.DMA((2 + REACH,)),
                pltpu.SemaphoreType.DMA((2,)),
                pltpu.SemaphoreType.DMA((4 * PLANE,)),
                pltpu.SemaphoreType.DMA((4 * PLANE,)),
                pltpu.SemaphoreType.DMA((2 * REACH,)),
                pltpu.SemaphoreType.DMA((2 * REACH,)),
                pltpu.SemaphoreType.DMA((PLANE + REACH,)),
                pltpu.SemaphoreType.DMA,
                pltpu.SemaphoreType.DMA,
            ],
            compiler_params=pltpu.CompilerParams(
                collective_id=0, has_side_effects=True, vmem_limit_bytes=63 * 2**20
            ),
        )(qk, value, pair_mask)
        return pl.pallas_call(
            hand_over,
            out_shape=jax.ShapeDtypeStruct((part, width), jnp.bfloat16),
            in_specs=[pl.BlockSpec(memory_space=pl.ANY)],
            out_specs=pl.BlockSpec(memory_space=pl.ANY),
            scratch_shapes=[
                pltpu.VMEM((part, width), jnp.bfloat16),
                pltpu.SemaphoreType.DMA((PIECES,)),
                pltpu.SemaphoreType.DMA((PIECES,)),
            ],
            compiler_params=pltpu.CompilerParams(vmem_limit_bytes=63 * 2**20),
        )(made)

    return jax.shard_map(
        local,
        mesh=mesh,
        in_specs=(P(("frame", "head"), None), P(("frame", "head"), None), P("frame", None)),
        out_specs=P(("frame", "head"), None),
        check_vma=False,
    )
```

```python
import functools
import math

import jax
import jax.numpy as jnp
from jax import lax
from jax.experimental import pallas as pl
from jax.experimental.pallas import tpu as pltpu
from jax.sharding import PartitionSpec as P

MESH = pl.DeviceIdType.MESH
DH = 128
PLANE = 8
REACH = 3
SPAN = 2 * REACH + 1
SLOTS = PLANE + 2 * REACH
COLS = 6
DEAD = 1e30
LATE = 2
PIECES = 3
V_STEP = 11
LOG2 = math.log2(math.e) / math.sqrt(DH)


def rows_of(slot, tok):
    return pl.ds(pl.multiple_of(slot * tok, tok), tok)


def wait_bytes(ref, sem):
    pltpu.make_async_copy(ref, ref, sem).wait()


def kernel(
    planes,
    qk_ref,
    value_ref,
    mask_ref,
    out_ref,
    kbuf,
    vbuf,
    mbuf,
    mine,
    listed,
    pbuf,
    sbuf,
    obuf,
    k_sent,
    v_sent,
    m_sent,
    o_sent,
    up_sent,
    down_sent,
    k_got,
    v_got,
    k_halo,
    v_halo,
    m_got,
    o_got,
    listed_got,
):
    part = qk_ref.shape[0]
    tok = 4 * part
    frame, x = lax.axis_index("frame"), lax.axis_index("head")
    z, phi = frame // PLANE, frame % PLANE
    base = frame - phi
    own_shift = 2 * (x % 2)
    seat = (phi - own_shift + PLANE) % PLANE
    active = seat % 4 != 3
    head = COLS * x + seat - seat // 4
    has_low, has_high = z > 0, z < planes - 1

    def place(x_to, j):
        return (j + j // 3 + 2 * (x_to % 2)) % PLANE

    row_copy = pltpu.make_async_copy(mask_ref, listed, listed_got)
    row_copy.start()

    barrier = pltpu.get_barrier_semaphore()

    def greet(i, c):
        f_to, x_to = i // 4, i % 4

        @pl.when(jnp.logical_or(f_to != phi, x_to != x))
        def _():
            pl.semaphore_signal(barrier, 1, device_id=(base + f_to, x_to), device_id_type=MESH)

        return c

    lax.fori_loop(0, 4 * PLANE, greet, 0)

    @pl.when(has_low)
    def _():
        pl.semaphore_signal(barrier, 1, device_id=(frame - PLANE, x), device_id_type=MESH)

    @pl.when(has_high)
    def _():
        pl.semaphore_signal(barrier, 1, device_id=(frame + PLANE, x), device_id_type=MESH)

    row_copy.wait()
    row = lax.broadcasted_iota(jnp.int32, mine.shape, 0)
    picked = jnp.where(row == 0, listed[0, 0], jnp.where(row == 1, listed[0, 1], listed[0, 2]))
    mine[...] = jnp.where(picked == 1, 0.0, DEAD).astype(jnp.float32)
    vbuf[:, DH:] = jnp.ones((SLOTS * tok, DH), jnp.bfloat16)

    @pl.when(jnp.logical_not(has_low))
    def _():
        kbuf[: REACH * tok, :] = jnp.zeros((REACH * tok, DH), jnp.bfloat16)
        vbuf[: REACH * tok, :DH] = jnp.zeros((REACH * tok, DH), jnp.bfloat16)
        for s in range(REACH):
            mbuf[s] = jnp.full(mine.shape, DEAD, jnp.float32)

    @pl.when(jnp.logical_not(has_high))
    def _():
        kbuf[(PLANE + REACH) * tok :, :] = jnp.zeros((REACH * tok, DH), jnp.bfloat16)
        vbuf[(PLANE + REACH) * tok :, :DH] = jnp.zeros((REACH * tok, DH), jnp.bfloat16)

    greeted = 4 * PLANE - 1 + has_low.astype(jnp.int32) + has_high.astype(jnp.int32)
    pl.semaphore_wait(barrier, greeted)

    def offset(i):
        i = (4 * PLANE - i) % (4 * PLANE)
        q, dx = i // 4, i % 4
        return dx, (q + dx) % 4, (q // 4 + dx) % 2

    def target(i):
        dx, dy, dc = offset(i)
        x_to = (x + dx) % 4
        f_to = (phi // 2 + dy) % 4 * 2 + (phi + dc) % 2
        seat_to = (f_to + 2 * PLANE - 2 * (x_to % 2)) % PLANE
        return x_to, f_to, seat_to % 4 != 3, COLS * x_to + seat_to - seat_to // 4

    def origin(i):
        dx, dy, dc = offset(i)
        return (x + 4 - dx) % 4, (phi // 2 + 4 - dy) % 4 * 2 + (phi + dc) % 2

    def chunk(f, x_of):
        return pl.ds(pl.multiple_of((REACH + f) * tok + part * x_of, part), part)

    def parcel(i, src, dst_at, sent, got):
        x_to, f_to, _, head_to = target(i)
        return pltpu.make_async_remote_copy(
            src_ref=src.at[:, pl.ds(pl.multiple_of(head_to * DH, DH), DH)],
            dst_ref=dst_at(chunk(phi, x)),
            send_sem=sent,
            recv_sem=got.at[i],
            device_id=(base + f_to, x_to),
            device_id_type=MESH,
        )

    def keep(src, dst_at, got):
        columns = pl.ds(pl.multiple_of(head * DH, DH), DH)
        pltpu.make_async_copy(src.at[:, columns], dst_at(chunk(phi, x)), got.at[0]).start()

    def k_at(rows):
        return kbuf.at[rows, :]

    def v_at(rows):
        return vbuf.at[rows, pl.ds(0, DH)]

    def give_mask(j, c):
        f_to = place(x, j)

        @pl.when(f_to == phi)
        def _():
            pltpu.make_async_copy(mine, mbuf.at[REACH + phi], m_got.at[REACH + phi]).start()

        @pl.when(f_to != phi)
        def _():
            pltpu.make_async_remote_copy(
                src_ref=mine,
                dst_ref=mbuf.at[REACH + phi],
                send_sem=m_sent,
                recv_sem=m_got.at[REACH + phi],
                device_id=(base + f_to, x),
                device_id_type=MESH,
            ).start()

        return c

    def qk_parcel(i):
        return parcel(i, qk_ref, k_at, k_sent.at[i], k_got)

    def value_parcel(i):
        return parcel(i, value_ref, v_at, v_sent, v_got)

    def send_qk(i, c):
        @pl.when(target(i)[2])
        def _():
            qk_parcel(i).start()

        return c

    def pass_on(i, ref_at, got, halo, kind):
        x_of, f = origin(i)
        here = ref_at(chunk(f, x_of))
        wait_bytes(here, got.at[i])

        @pl.when(jnp.logical_and(f >= PLANE - REACH, has_high))
        def _():
            pltpu.make_async_remote_copy(
                src_ref=here,
                dst_ref=ref_at(chunk(f - PLANE, x_of)),
                send_sem=up_sent.at[kind],
                recv_sem=halo.at[f - PLANE + REACH],
                device_id=(frame + PLANE, x),
                device_id_type=MESH,
            ).start()

        @pl.when(jnp.logical_and(f < REACH, has_low))
        def _():
            pltpu.make_async_remote_copy(
                src_ref=here,
                dst_ref=ref_at(chunk(f + PLANE, x_of)),
                send_sem=down_sent.at[kind],
                recv_sem=halo.at[f + REACH],
                device_id=(frame - PLANE, x),
                device_id_type=MESH,
            ).start()

    def exchange(i, c):
        @pl.when(jnp.logical_and(target(i)[2], i > 0))
        def _():
            qk_parcel(i).wait_send()
            value_parcel(i).start()

        @pl.when(active)
        def _():
            pass_on(i, k_at, k_got, k_halo, 0)

        return c

    lax.fori_loop(0, COLS, give_mask, 0)
    lax.fori_loop(1, 4 * PLANE, send_qk, 0)

    @pl.when(active)
    def _():
        keep(qk_ref, k_at, k_got)
        keep(value_ref, v_at, v_got)

    def mask_up(n):
        return pltpu.make_async_remote_copy(
            src_ref=mbuf.at[REACH + PLANE - 1 - n],
            dst_ref=mbuf.at[REACH - 1 - n],
            send_sem=up_sent.at[2 + n],
            recv_sem=m_got.at[REACH - 1 - n],
            device_id=(frame + PLANE, x),
            device_id_type=MESH,
        )

    def frame_at(i):
        return jnp.where((i + x) % 2 == 0, PLANE // 2 - 1 - i // 2, PLANE // 2 + i // 2)

    def wait_halo(f, ref_at, halo):
        low = f < PLANE // 2
        slot = jnp.where(low, f, f + 2 * REACH)
        index = jnp.where(low, f, f - PLANE + 2 * REACH)

        @pl.when(jnp.where(low, has_low, has_high))
        def _():
            wait_bytes(ref_at(rows_of(slot, tok)), halo.at[index])

    def weigh(f):
        q = kbuf[rows_of(f + REACH, tok), :]
        bias = []
        for g in range(SPAN):
            k = g - REACH
            if k < 0:
                bias.append(mbuf[REACH + f + k, pl.ds(-k - 1, 1), :])
            elif k == 0:
                bias.append(None)
            else:
                given = mbuf[REACH + f, pl.ds(k - 1, 1), :]
                bias.append(jnp.where(jnp.logical_or(has_high, f + k < PLANE), given, DEAD))
        best = None
        for g in range(SPAN):
            k = kbuf[rows_of(f + g, tok), :]
            s = lax.dot_general(q, k, (((1,), (1,)), ((), ())), preferred_element_type=jnp.float32)
            if g == REACH:
                first = lax.broadcasted_iota(jnp.int32, s.shape, 0)
                second = lax.broadcasted_iota(jnp.int32, s.shape, 1)
                s = jnp.where(first == second, -DEAD, s)
            sbuf[:, g * tok : (g + 1) * tok] = s
            t = functools.reduce(jnp.maximum, [s[:, c : c + DH] for c in range(0, tok, DH)])
            if g != REACH:
                t = t - bias[g]
            best = t if best is None else jnp.maximum(best, t)
        best = jnp.broadcast_to(jnp.max(best, axis=1, keepdims=True) * LOG2, (tok, DH))
        for g in range(SPAN):
            less = best if g == REACH else best + bias[g]
            for c in range(g * tok, (g + 1) * tok, DH):
                pbuf[f, :, c : c + DH] = jnp.exp2(sbuf[:, c : c + DH] * LOG2 - less).astype(jnp.bfloat16)

    def give_out(f, x_to, here):
        rows = pl.ds(pl.multiple_of(f * tok + x_to * part, part), part)
        columns = pl.ds(pl.multiple_of(head * DH, DH), DH)

        @pl.when(here)
        def _():
            pltpu.make_async_copy(obuf.at[rows, :], out_ref.at[:, columns], o_got).start()

        @pl.when(jnp.logical_not(here))
        def _():
            pltpu.make_async_remote_copy(
                src_ref=obuf.at[rows, :],
                dst_ref=out_ref.at[:, columns],
                send_sem=o_sent,
                recv_sem=o_got,
                device_id=(base + f, x_to),
                device_id_type=MESH,
            ).start()

    lax.fori_loop(0, PLANE, exchange, 0)

    @pl.when(active)
    def _():
        for n in range(PLANE):
            wait_bytes(mbuf.at[REACH + n], m_got.at[REACH + n])
        for n in range(REACH):

            @pl.when(has_high)
            def _():
                mask_up(n).start()

    lax.fori_loop(PLANE, 4 * PLANE, exchange, 0)

    @pl.when(active)
    def _():
        def scores_step(i, c):
            f = frame_at(i)

            @pl.when(i >= 2)
            def _():
                wait_halo(f, k_at, k_halo)

            @pl.when(jnp.logical_and(i == 2, has_low))
            def _():
                for n in range(REACH):
                    wait_bytes(mbuf.at[n], m_got.at[n])

            weigh(f)

            def hand_on(n, c):
                pass_on(n, v_at, v_got, v_halo, 1)
                return c

            lax.fori_loop(V_STEP * i, jnp.minimum(V_STEP * (i + 1), 4 * PLANE), hand_on, 0)
            return c

        lax.fori_loop(0, PLANE, scores_step, 0)

        def value_step(i, c):
            rest = PLANE - LATE
            f = frame_at(jnp.where(i < LATE, i, LATE + (i - LATE + 2 * ((phi // 2 + x) % 3)) % rest))

            @pl.when(i == LATE)
            def _():
                for n in range(LATE, PLANE):
                    wait_halo(frame_at(n), v_at, v_halo)

            values = vbuf[pl.ds(pl.multiple_of(f * tok, tok), SPAN * tok), :]
            o = jnp.dot(pbuf[f], values, preferred_element_type=jnp.float32)
            obuf[rows_of(f, tok), :] = (o[:, :DH] / o[:, DH:]).astype(jnp.bfloat16)
            for n in (2, 1, 3, 0):
                give_out(f, (x + n) % 4, jnp.logical_and(f == phi, n == 0))
            return c

        lax.fori_loop(0, PLANE, value_step, 0)

        wait_bytes(value_ref.at[:, pl.ds(0, (4 * COLS - 1) * DH)], v_sent)
        wait_bytes(mbuf.at[pl.ds(0, COLS - 1)], m_sent)
        wait_bytes(obuf.at[pl.ds(0, (4 * PLANE - 1) * part), :], o_sent)

        @pl.when(has_high)
        def _():
            wait_bytes(kbuf.at[pl.ds(0, REACH * tok), :], up_sent.at[0])
            wait_bytes(v_at(pl.ds(0, REACH * tok)), up_sent.at[1])
            for n in range(REACH):
                mask_up(n).wait_send()

        @pl.when(has_low)
        def _():
            wait_bytes(kbuf.at[pl.ds(0, REACH * tok), :], down_sent.at[0])
            wait_bytes(v_at(pl.ds(0, REACH * tok)), down_sent.at[1])

    @pl.when(jnp.logical_not(active))
    def _():
        wait_bytes(value_ref, v_sent)
        wait_bytes(mbuf.at[pl.ds(0, COLS)], m_sent)

    wait_bytes(out_ref, o_got)


def hand_over(src, dst, buffer, came, went):
    step = src.shape[0] // PIECES
    into, out = [], []
    for n in range(PIECES):
        rows = pl.ds(n * step, step)
        into.append(pltpu.make_async_copy(src.at[rows, :], buffer.at[rows, :], came.at[n]))
        out.append(pltpu.make_async_copy(buffer.at[rows, :], dst.at[rows, :], went.at[n]))
    for copy in into:
        copy.start()
    for first, second in zip(into, out):
        first.wait()
        second.start()
    for copy in out:
        copy.wait()


def solution(mesh):
    planes = mesh.shape["frame"] // PLANE

    def local(qk, value, pair_mask):
        part, width = qk.shape
        tok = 4 * part
        made = pl.pallas_call(
            functools.partial(kernel, planes),
            out_shape=jax.ShapeDtypeStruct((part, width), jnp.bfloat16),
            in_specs=[
                pl.BlockSpec(memory_space=pl.ANY),
                pl.BlockSpec(memory_space=pl.ANY),
                pl.BlockSpec(memory_space=pl.ANY),
            ],
            out_specs=pl.BlockSpec(memory_space=pl.ANY),
            scratch_shapes=[
                pltpu.VMEM((SLOTS * tok, DH), jnp.bfloat16),
                pltpu.VMEM((SLOTS * tok, 2 * DH), jnp.bfloat16),
                pltpu.VMEM((PLANE + REACH, 8, DH), jnp.float32),
                pltpu.VMEM((8, DH), jnp.float32),
                pltpu.SMEM((1, REACH), jnp.int32),
                pltpu.VMEM((PLANE, tok, SPAN * tok), jnp.bfloat16),
                pltpu.VMEM((tok, SPAN * tok), jnp.float32),
                pltpu.VMEM((PLANE * tok, DH), jnp.bfloat16),
                pltpu.SemaphoreType.DMA((4 * PLANE,)),
                pltpu.SemaphoreType.DMA,
                pltpu.SemaphoreType.DMA,
                pltpu.SemaphoreType.DMA,
                pltpu.SemaphoreType.DMA((2 + REACH,)),
                pltpu.SemaphoreType.DMA((2,)),
                pltpu.SemaphoreType.DMA((4 * PLANE,)),
                pltpu.SemaphoreType.DMA((4 * PLANE,)),
                pltpu.SemaphoreType.DMA((2 * REACH,)),
                pltpu.SemaphoreType.DMA((2 * REACH,)),
                pltpu.SemaphoreType.DMA((PLANE + REACH,)),
                pltpu.SemaphoreType.DMA,
                pltpu.SemaphoreType.DMA,
            ],
            compiler_params=pltpu.CompilerParams(
                collective_id=0, has_side_effects=True, vmem_limit_bytes=63 * 2**20
            ),
        )(qk, value, pair_mask)
        return pl.pallas_call(
            hand_over,
            out_shape=jax.ShapeDtypeStruct((part, width), jnp.bfloat16),
            in_specs=[pl.BlockSpec(memory_space=pl.ANY)],
            out_specs=pl.BlockSpec(memory_space=pl.ANY),
            scratch_shapes=[
                pltpu.VMEM((part, width), jnp.bfloat16),
                pltpu.SemaphoreType.DMA((PIECES,)),
                pltpu.SemaphoreType.DMA((PIECES,)),
            ],
            compiler_params=pltpu.CompilerParams(vmem_limit_bytes=63 * 2**20),
        )(made)

    return jax.shard_map(
        local,
        mesh=mesh,
        in_specs=(P(("frame", "head"), None), P(("frame", "head"), None), P("frame", None)),
        out_specs=P(("frame", "head"), None),
        check_vma=False,
    )
```
